256 devices in a mesh: lat: 4 (over x_lo, core), lon: 64 (over z, y, x_hi).
Axes of the slice: x: 4 (x_hi: 2, x_lo: 2; x = x_hi * 2 + x_lo), y: 4, z: 8, core: 2. Of those that a mesh axis runs over, the one named last changes fastest.
Arguments:
- tokens: bfloat16 [64, 1024, 1536], P('lat', 'lon'), may hold values from -6 to 6
- cotangent: bfloat16 [64, 1024, 1536], P('lat', 'lon'), may hold values from -6 to 6
- gain: float32 [1536], replicated, may hold values from 0.5 to 1.5
- w_qkv: bfloat16 [1536, 4608], P('lon'), may hold values from -0.15625 to 0.15625
- w_out: bfloat16 [1536, 1536], P('lon'), may hold values from -0.15625 to 0.15625
- logit_scale: float32 [24], replicated, may hold values from 2 to 12
- region_ids: int32 [64, 1024], P('lat', 'lon'), may hold values from 0 to 2
Outputs:
- output: bfloat16 [64, 1024, 1536], P('lat', 'lon')
- grad_input: bfloat16 [64, 1024, 1536], P('lat', 'lon')
The draws below stay inside these ranges and needn't reach their ends.
All inputs are finite; a program needn't handle non-finite values.
Results may differ from the reference program's by a relative error of at most 0.0071.
Values may be sent and summed in bfloat16 or wider, within the bound.
No kernel may reach another device: no remote copies, remote signals or barrier semaphores. Data moves between devices by JAX's collectives and lax.ppermute only.
A program may use at most 128 MiB of HBM per device.

```python
import math
import jax
import jax.numpy as jnp
from jax import lax

D = 1536
HEADS = 24
HEAD_DIM = 64
WIN_LAT = 4
WIN_LON = 16
SHIFT_LAT = 2
SHIFT_LON = 8
NLAT = 64
NLON = 1024


def with_ends(values, own_key, low, high):
    shape = values.shape
    place = [jax.random.randint(jax.random.fold_in(own_key, axis), (), 0, shape[axis]) for axis in range(len(shape))]
    values = values.at[tuple(place)].set(low)
    longest = shape.index(max(shape))
    place[longest] = (place[longest] + 1) % shape[longest]
    return values.at[tuple(place)].set(high)


def block_levels(key, extent, split, smallest, top_value):
    def one(dim, blocks):
        steps = jax.random.uniform(jax.random.fold_in(jax.random.fold_in(key, 6), dim), (blocks,), jnp.float32, smallest / len(split), top_value / len(split))
        return jnp.repeat(jnp.exp(steps), extent[dim] // blocks).reshape((-1,) + (1,) * (len(extent) - dim - 1))

    level = one(*split[0])
    for cut in split[1:]:
        level = level * one(*cut)
    return level


def normal_values(key, shape, scale, bound, cuts=(), kind=jnp.bfloat16):
    drawn = jax.random.normal(key, shape, jnp.float32) * scale
    if len(cuts) > 0:
        drawn = block_levels(key, shape, cuts, -0.22, 0.18) * drawn
    return jnp.clip(drawn, min=-bound, max=bound).astype(kind)


def setup_inputs(seed: int = 0) -> dict:
    key_list = jax.random.split(jax.random.key(seed), 8)
    tokens = normal_values(key_list[0], (NLAT, NLON, D), 1.0, 6.0, ((0, 4), (1, 64)))
    cotangent = normal_values(key_list[1], (NLAT, NLON, D), 1.0, 6.0, ((0, 4), (1, 64)))
    gain = jnp.clip(1.0 + 0.1 * jax.random.normal(key_list[2], (D,), jnp.float32), 0.5, 1.5)
    w_qkv = normal_values(key_list[3], (D, 3 * HEADS * HEAD_DIM), D ** -0.5, 0.15625, ((0, 64),))
    w_out = normal_values(key_list[4], (HEADS * HEAD_DIM, D), (HEADS * HEAD_DIM) ** -0.5, 0.15625, ((0, 64),))
    logit_scale = jnp.clip(jnp.exp(jax.random.uniform(key_list[5], (HEADS,), jnp.float32, math.log(2.0), math.log(12.0))), 2.0, 12.0)
    region_ids = with_ends(jax.random.randint(key_list[6], (NLAT, NLON), 0, 3), jax.random.fold_in(key_list[6], 1), 0, 2).astype(jnp.int32)
    return dict(tokens=tokens, cotangent=cotangent, gain=gain, w_qkv=w_qkv, w_out=w_out, logit_scale=logit_scale, region_ids=region_ids)


def layer_norm(tokens_f32, gain):
    centre = tokens_f32 - lax.optimization_barrier(jnp.mean(tokens_f32, axis=-1, keepdims=True))
    spread = lax.optimization_barrier(jnp.mean(centre * centre, axis=-1, keepdims=True))
    return (centre * lax.rsqrt(spread + 1e-05) * gain).astype(jnp.bfloat16)

def to_windows(tensor):
    span_lat, span_lon, features = tensor.shape
    shaped = tensor.reshape(span_lat // WIN_LAT, WIN_LAT, span_lon // WIN_LON, WIN_LON, features)
    return shaped.transpose(0, 2, 1, 3, 4).reshape(-1, WIN_LAT * WIN_LON, features)

def from_windows(blocks, span_lat, span_lon):
    features = blocks.shape[-1]
    shaped = blocks.reshape(span_lat // WIN_LAT, span_lon // WIN_LON, WIN_LAT, WIN_LON, features)
    return shaped.transpose(0, 2, 1, 3, 4).reshape(span_lat, span_lon, features)

def window_attend(blocks, region_win, valid_win, w_qkv, logit_scale):
    count_win, count_tok, model_dim = blocks.shape
    heads_num = logit_scale.shape[0]
    head_size = w_qkv.shape[1] // (3 * heads_num)
    packed_half = jnp.dot(blocks.reshape(-1, model_dim), w_qkv, preferred_element_type=jnp.float32).astype(jnp.bfloat16)
    packed_half = lax.optimization_barrier(packed_half).reshape(count_win, count_tok, 3, heads_num, head_size)
    values = packed_half[:, :, 2]
    packed = packed_half.astype(jnp.float32)
    queries = packed[:, :, 0]
    keys_all = packed[:, :, 1]
    queries = queries * lax.rsqrt(lax.optimization_barrier(jnp.sum(queries * queries, axis=-1, keepdims=True)) + 1e-06)
    keys_all = keys_all * lax.rsqrt(lax.optimization_barrier(jnp.sum(keys_all * keys_all, axis=-1, keepdims=True)) + 1e-06)
    scores = jnp.einsum('bqhe,bkhe->bhqk', queries, keys_all, precision=lax.Precision.HIGHEST)
    scores = scores * logit_scale[None, :, None, None]
    allowed = (region_win[:, :, None] == region_win[:, None, :]) & (valid_win[:, None, :] | jnp.eye(count_tok, dtype=bool)[None])
    weights = jnp.where(allowed[:, None], jnp.exp(scores), 0.0)
    probs = (weights / lax.optimization_barrier(jnp.sum(weights, axis=-1, keepdims=True))).astype(jnp.bfloat16)
    probs = lax.optimization_barrier(probs)
    mixed = jnp.einsum('bhqk,bkhe->bqhe', probs, values, preferred_element_type=jnp.float32)
    return mixed.reshape(count_win, count_tok, heads_num * head_size).astype(jnp.bfloat16)

def project(mixed, w_out):
    leading = mixed.shape[:-1]
    result = jnp.dot(mixed.reshape(-1, mixed.shape[-1]), w_out, preferred_element_type=jnp.float32)
    return result.astype(jnp.bfloat16).reshape(leading + (w_out.shape[1],))

def project_back(upstream, w_out):
    leading = upstream.shape[:-1]
    result = lax.dot_general(upstream.reshape(-1, upstream.shape[-1]), w_out, (((1,), (1,)), ((), ())), preferred_element_type=jnp.float32)
    return result.astype(jnp.bfloat16).reshape(leading + (w_out.shape[0],))

def reference(tokens, cotangent, gain, w_qkv, w_out, logit_scale, region_ids):
    total_lat, total_lon, model_dim = tokens.shape
    tokens_f32 = tokens.astype(jnp.float32)
    normed, norm_back = jax.vjp(lambda inner: layer_norm(inner, gain), tokens_f32)

    def ahead(tensor):
        rolled = jnp.roll(tensor, -SHIFT_LON, axis=1)
        return jnp.concatenate([rolled[SHIFT_LAT:], jnp.zeros_like(rolled[:SHIFT_LAT])], axis=0)

    def behind(tensor):
        rolled = jnp.roll(tensor, SHIFT_LON, axis=1)
        return jnp.concatenate([jnp.zeros_like(rolled[:SHIFT_LAT]), rolled[:-SHIFT_LAT]], axis=0)
    shifted = ahead(normed)
    row_index = lax.broadcasted_iota(jnp.int32, (total_lat, total_lon, 1), 0)
    valid_win = to_windows(row_index + SHIFT_LAT < total_lat)[..., 0]
    region_win = to_windows(region_ids[..., None])[..., 0]
    attended, attend_back = jax.vjp(lambda inner: window_attend(inner, region_win, valid_win, w_qkv, logit_scale), to_windows(shifted))
    update = behind(from_windows(project(attended, w_out), total_lat, total_lon))
    update = lax.optimization_barrier(update)
    output = (tokens_f32 + update.astype(jnp.float32)).astype(jnp.bfloat16)
    upstream = to_windows(ahead(cotangent))
    grad_mixed = project_back(upstream, w_out)
    grad_win, = attend_back(grad_mixed)
    grad_normed = behind(from_windows(grad_win, total_lat, total_lon))
    grad_tokens, = norm_back(grad_normed)
    grad_input = (grad_tokens + cotangent.astype(jnp.float32)).astype(jnp.bfloat16)
    return (output, grad_input)
```

```python
import functools
import itertools

import jax
import jax.numpy as jnp
from jax import lax
from jax.experimental import pallas as pl
from jax.experimental.pallas import tpu as pltpu
from jax.sharding import Mesh
from jax.sharding import PartitionSpec as P

SHIFT_LAT = 2
SHIFT_LON = 8
D = 1536
SIZES = {"xl": 2, "core": 2, "z": 8, "y": 4, "xh": 2}
AXES = tuple(SIZES)
LAT = ("xl", "core")
LON = ("z", "y", "xh")
TOK = 256
WIN = 64
PAIRS = 12
Y_ORDER = (0, 1, -1, 2)
Z_ORDER = (0, 1, -1, 2, -2, 3, -3, 4)
UNITS = 32
UROWS = 48


def linear(place, axes):
    total = 0
    for axis in axes:
        total = total * SIZES[axis] + place[axis]
    return total


def permutation(target):
    pairs = []
    for values in itertools.product(*[range(SIZES[axis]) for axis in AXES]):
        place = dict(zip(AXES, values))
        goal = target(dict(place))
        if goal is not None:
            pairs.append((linear(place, AXES), linear(goal, AXES)))
    return pairs


def along(axis, step):
    def target(place):
        place[axis] = (place[axis] + step) % SIZES[axis]
        return place

    return permutation(target)


def across_x():
    def target(place):
        x = 3 - (place["xh"] * 2 + place["xl"])
        place["xh"], place["xl"] = x // 2, x % 2
        return place

    return permutation(target)


def send(value, pairs):
    return lax.ppermute(value, AXES, pairs)


def lon_ring(value, step):
    size = SIZES["z"] * SIZES["y"] * SIZES["xh"]
    return lax.ppermute(value, LON, [(i, (i + step) % size) for i in range(size)])


def lat_line(value, step):
    size = SIZES["xl"] * SIZES["core"]
    return lax.ppermute(
        value, LAT, [(i, i + step) for i in range(size) if 0 <= i + step < size]
    )


def both_ways(block, axis):
    size = SIZES[axis]
    got = []
    ahead = behind = block
    for step in range(1, size // 2):
        ahead = send(ahead, along(axis, 1))
        behind = send(behind, along(axis, -1))
        got += [(step, None, ahead), (-step, None, behind)]
    half = block.shape[-1] // 2
    got.append((size // 2, 0, send(ahead[..., :half], along(axis, 1))))
    got.append((size // 2, 1, send(behind[..., half:], along(axis, -1))))
    return got


def gather_weights(w_qkv, w_out):
    core = lax.axis_index("core")
    x_hi = lax.axis_index("xh")
    first = jnp.where(core == 0, w_qkv[:, :D], w_qkv[:, 2 * D :])
    second = jnp.where(core == 0, w_qkv[:, D : 2 * D], w_out)

    def cross(block):
        other = send(block, across_x())
        low = jnp.where(x_hi == 0, block, other)
        high = jnp.where(x_hi == 0, other, block)
        return jnp.concatenate([low, high])[None]

    first, second = cross(first), cross(second)
    first = jnp.concatenate([first] + [send(first, along("y", s)) for s in Y_ORDER[1:]])
    ahead = behind = second
    parts = [second]
    for _ in range(1, SIZES["z"] // 2):
        ahead = send(ahead, along("z", 1))
        behind = send(behind, along("z", -1))
        parts += [ahead, behind]
    parts.append(send(ahead, along("z", 1)))
    second = jnp.concatenate(parts)
    own = [(0, step, half, block) for step, half, block in [(0, None, first)] + both_ways(first, "z")]
    own += [(1, step, half, block) for step, half, block in [(0, None, second)] + both_ways(second, "y")]
    plan, blocks = [], []
    for kind, step, half, block in own:
        plan += [(kind, step, half, 0), (kind, step, half, 1)]
        blocks += [block, send(block, along("core", 1))]
    return plan, blocks


def pull_ahead(tensor):
    edge = lon_ring(tensor[:, :, :SHIFT_LON], -1)
    widened = jnp.concatenate([tensor[:, :, SHIFT_LON:], edge], axis=2)
    rim = lat_line(widened[:, :SHIFT_LAT], -1)
    return jnp.concatenate([widened[:, SHIFT_LAT:], rim], axis=1)


def pull_behind(tensor):
    edge = lon_ring(tensor[:, :, -SHIFT_LON:], 1)
    widened = jnp.concatenate([edge, tensor[:, :, :-SHIFT_LON]], axis=2)
    rim = lat_line(widened[:, -SHIFT_LAT:], 1)
    return jnp.concatenate([rim, widened[:, :-SHIFT_LAT]], axis=1)


def mm(a, b):
    return lax.dot_general(a, b, (((1,), (0,)), ((), ())), preferred_element_type=jnp.float32)


def mm_nt(a, b):
    return lax.dot_general(a, b, (((1,), (1,)), ((), ())), preferred_element_type=jnp.float32)


def mm_tn(a, b):
    return lax.dot_general(a, b, (((0,), (0,)), ((), ())), preferred_element_type=jnp.float32)


def bf(value):
    return value.astype(jnp.bfloat16)


def sum_heads(value, ones):
    high = bf(value)
    low = bf(value - high.astype(jnp.float32))
    return mm(high, ones) + mm(low, ones)


def window_kernel(plan, pos, xs, gs, mask, gain, scale, *refs):
    count = len(plan)
    blocks = refs[:count]
    upd, gwin = refs[count : count + 2]
    weights, normed, gatt, packed, attended, sem = refs[count + 2 :]
    z, y, core = pos[0], pos[1], pos[2]

    copies = 0
    for (kind, step, half, other), block in zip(plan, blocks):
        side = lax.rem(core + other, 2)
        matrix = 2 * side + kind
        cols = slice(None) if half is None else pl.ds(half * (D // 2), D // 2)
        for j, offset in enumerate(Y_ORDER if kind == 0 else Z_ORDER):
            dz, dy = (step, offset) if kind == 0 else (offset, step)
            unit = lax.rem(z - dz + 8, 8) * 4 + lax.rem(y - dy + 4, 4)
            pltpu.make_async_copy(block.at[j], weights.at[matrix, unit, :, cols], sem.at[copies]).start()
            copies += 1

    for i in range(4):
        rows = pl.ds(i * WIN, WIN)
        x = xs[rows, :].astype(jnp.float32)
        centre = x - jnp.mean(x, axis=-1, keepdims=True)
        spread = jnp.mean(centre * centre, axis=-1, keepdims=True)
        normed[rows, :] = bf(centre * lax.rsqrt(spread + 1e-05) * gain[...])

    copies = 0
    for (kind, step, half, other), block in zip(plan, blocks):
        cols = slice(None) if half is None else pl.ds(half * (D // 2), D // 2)
        for j in range(block.shape[0]):
            pltpu.make_async_copy(block.at[j], weights.at[0, 0, :, cols], sem.at[copies]).wait()
            copies += 1

    @pl.loop(0, 2)
    def _(i):
        w = weights[3, pl.ds(i * 16, 16)].reshape(768, D)
        gatt[:, pl.ds(pl.multiple_of(i * 768, 128), 768)] = bf(mm_nt(gs[...], w))

    @pl.loop(0, 3)
    def _(m):
        @pl.loop(0, 3)
        def _(i):
            w = weights[m, :, :, pl.ds(pl.multiple_of(i * 512, 128), 512)].reshape(D, 512)
            packed[:, pl.ds(pl.multiple_of(m * D + i * 512, 128), 512)] = bf(mm(normed[...], w))

    lane = lax.broadcasted_iota(jnp.int32, (128, 128), 1)
    row = lax.broadcasted_iota(jnp.int32, (128, 128), 0)
    same = (lane < 64) == (row < 64)
    ones = jnp.where(same, 1.0, 0.0).astype(jnp.bfloat16)
    left = lax.broadcasted_iota(jnp.int32, (WIN, 128), 1) < 64

    def spread_heads(block):
        zero = jnp.zeros_like(block)
        return jnp.concatenate([jnp.where(left, block, zero), jnp.where(left, zero, block)], axis=0)

    def fold_heads(block):
        return jnp.where(left, block[:WIN], block[WIN:])

    @pl.loop(0, PAIRS)
    def _(p):
        at_q = pl.ds(pl.multiple_of(p * 128, 128), 128)
        at_k = pl.ds(pl.multiple_of(D + p * 128, 128), 128)
        at_v = pl.ds(pl.multiple_of(2 * D + p * 128, 128), 128)
        q = packed[:, at_q].astype(jnp.float32)
        k = packed[:, at_k].astype(jnp.float32)
        rq = lax.rsqrt(sum_heads(q * q, ones) + 1e-06)
        rk = lax.rsqrt(sum_heads(k * k, ones) + 1e-06)
        qn, kn = q * rq, k * rk
        qb, kb = bf(qn), bf(kn)
        factor = scale[pl.ds(p, 1), :]
        dqs, dks = [], []
        for i in range(4):
            rows = pl.ds(i * WIN, WIN)
            part = slice(i * WIN, (i + 1) * WIN)
            k2 = spread_heads(kb[part])
            v2 = spread_heads(packed[rows, at_v])
            d_out = gatt[rows, at_q]
            weight = jnp.exp(mm_nt(qb[part], k2) * factor) * mask[rows, :]
            prob = weight / sum_heads(weight, ones)
            prob16 = bf(prob)
            attended[rows, at_q] = bf(mm(prob16, v2))
            d_prob = mm_nt(d_out, v2)
            d_score = bf(prob * (d_prob - sum_heads(prob * d_prob, ones)) * factor)
            packed[rows, at_v] = bf(fold_heads(mm_tn(prob16, d_out)))
            dqs.append(mm(d_score, k2))
            dks.append(fold_heads(mm_tn(d_score, qb[part])))
        dq = jnp.concatenate(dqs, axis=0)
        dk = jnp.concatenate(dks, axis=0)
        packed[:, at_q] = bf(rq * (dq - qn * sum_heads(qn * dq, ones)))
        packed[:, at_k] = bf(rk * (dk - kn * sum_heads(kn * dk, ones)))

    @pl.loop(0, 3)
    def _(i):
        at = pl.ds(pl.multiple_of(i * 512, 128), 512)
        upd[:, at] = bf(mm(attended[...], weights[3, :, :, at].reshape(D, 512)))

    @pl.loop(0, 2)
    def _(i):
        total = mm_nt(packed[:, :D], weights[0, pl.ds(i * 16, 16)].reshape(768, D))
        total += mm_nt(packed[:, D : 2 * D], weights[1, pl.ds(i * 16, 16)].reshape(768, D))
        total += mm_nt(packed[:, 2 * D :], weights[2, pl.ds(i * 16, 16)].reshape(768, D))
        gwin[:, pl.ds(pl.multiple_of(i * 768, 128), 768)] = bf(total)


def window_attention(pos, xs, gs, mask, gain, scale, plan, blocks):
    vmem = pl.BlockSpec(memory_space=pltpu.VMEM)
    copies = sum(block.shape[0] for block in blocks)
    return pl.pallas_call(
        functools.partial(window_kernel, plan),
        out_shape=[jax.ShapeDtypeStruct((TOK, D), jnp.bfloat16)] * 2,
        in_specs=[pl.BlockSpec(memory_space=pltpu.SMEM)]
        + [vmem] * 5
        + [pl.BlockSpec(memory_space=pl.ANY)] * len(blocks),
        out_specs=[vmem, vmem],
        scratch_shapes=[
            pltpu.VMEM((4, UNITS, UROWS, D), jnp.bfloat16),
            pltpu.VMEM((TOK, D), jnp.bfloat16),
            pltpu.VMEM((TOK, D), jnp.bfloat16),
            pltpu.VMEM((TOK, 3 * D), jnp.bfloat16),
            pltpu.VMEM((TOK, D), jnp.bfloat16),
            pltpu.SemaphoreType.DMA((copies,)),
        ],
        compiler_params=pltpu.CompilerParams(vmem_limit_bytes=56 * 1024 * 1024),
        cost_estimate=pl.CostEstimate(
            flops=11 * 10**9, bytes_accessed=24 * 10**6, transcendentals=2 * 10**6
        ),
        name="window_attention",
    )(pos, xs, gs, mask, gain, scale, *blocks)


def finish_kernel(tokens, cotangent, update, grad, gain, out, grad_in):
    for i in range(4):
        rows = pl.ds(i * WIN, WIN)
        x = tokens[rows, :].astype(jnp.float32)
        out[rows, :] = bf(x + update[rows, :].astype(jnp.float32))
        centre = x - jnp.mean(x, axis=-1, keepdims=True)
        r = lax.rsqrt(jnp.mean(centre * centre, axis=-1, keepdims=True) + 1e-05)
        unit = centre * r
        g = grad[rows, :].astype(jnp.float32) * gain[...]
        pull = g - jnp.mean(g, axis=-1, keepdims=True)
        pull -= unit * jnp.mean(g * unit, axis=-1, keepdims=True)
        grad_in[rows, :] = bf(pull * r + cotangent[rows, :].astype(jnp.float32))


def finish(tokens, cotangent, update, grad, gain):
    vmem = pl.BlockSpec(memory_space=pltpu.VMEM)
    return pl.pallas_call(
        finish_kernel,
        out_shape=[jax.ShapeDtypeStruct((TOK, D), jnp.bfloat16)] * 2,
        in_specs=[vmem] * 5,
        out_specs=[vmem, vmem],
        compiler_params=pltpu.CompilerParams(vmem_limit_bytes=32 * 1024 * 1024),
        name="finish",
    )(tokens, cotangent, update, grad, gain)


def body(tokens, cotangent, gain, w_qkv, w_out, logit_scale, region_ids):
    lat, lon, _ = tokens.shape
    plan, blocks = gather_weights(w_qkv, w_out)
    shifted = pull_ahead(jnp.stack([tokens, cotangent]))
    shifted = shifted.reshape(2, TOK, D)
    gain = gain[None]
    scale = jnp.repeat(logit_scale, 64).reshape(PAIRS, 128)
    region = region_ids.reshape(4, WIN)
    row = lax.axis_index(LAT) * lat + lax.broadcasted_iota(jnp.int32, (lat, lon), 0)
    total_lat = lat * SIZES["xl"] * SIZES["core"]
    valid = (row + SHIFT_LAT < total_lat).reshape(4, WIN)
    allowed = (region[:, :, None] == region[:, None, :]) & (
        valid[:, None, :] | jnp.eye(WIN, dtype=bool)[None]
    )
    mask = allowed.astype(jnp.float32).reshape(TOK, WIN)
    mask = jnp.concatenate([mask, mask], axis=1)
    pos = jnp.stack([lax.axis_index("z"), lax.axis_index("y"), lax.axis_index("core")]).astype(jnp.int32)
    update, grad = window_attention(pos, shifted[0], shifted[1], mask, gain, scale, plan, blocks)
    update = pull_behind(update.reshape(1, lat, lon, D)).reshape(TOK, D)
    grad = pull_behind(grad.reshape(1, lat, lon, D)).reshape(TOK, D)
    output, grad_input = finish(
        tokens.reshape(TOK, D), cotangent.reshape(TOK, D), update, grad, gain
    )
    return output.reshape(lat, lon, D), grad_input.reshape(lat, lon, D)


def solution(mesh):
    fine = Mesh(mesh.devices.reshape(tuple(SIZES.values())), AXES)
    grid = P(LAT, LON, None)
    return jax.shard_map(
        body,
        mesh=fine,
        in_specs=(grid, grid, P(), P(LON, None), P(LON, None), P(), P(LAT, LON)),
        out_specs=(grid, grid),
        check_vma=False,
    )
```

```python
import functools
import itertools

import jax
import jax.numpy as jnp
from jax import lax
from jax.experimental import pallas as pl
from jax.experimental.pallas import tpu as pltpu
from jax.sharding import Mesh
from jax.sharding import PartitionSpec as P

SHIFT_LAT = 2
SHIFT_LON = 8
D = 1536
SIZES = {"xl": 2, "core": 2, "z": 8, "y": 4, "xh": 2}
AXES = tuple(SIZES)
LAT = ("xl", "core")
LON = ("z", "y", "xh")
TOK = 256
WIN = 64
PAIRS = 12
Y_ORDER = (0, 1, -1, 2)
CUT = 1024
UNITS = 32
UROWS = 48


def linear(place, axes):
    total = 0
    for axis in axes:
        total = total * SIZES[axis] + place[axis]
    return total


def permutation(target):
    pairs = []
    for values in itertools.product(*[range(SIZES[axis]) for axis in AXES]):
        place = dict(zip(AXES, values))
        goal = target(dict(place))
        if goal is not None:
            pairs.append((linear(place, AXES), linear(goal, AXES)))
    return pairs


def along(axis, step):
    def target(place):
        place[axis] = (place[axis] + step) % SIZES[axis]
        return place

    return permutation(target)


def across_x():
    def target(place):
        x = 3 - (place["xh"] * 2 + place["xl"])
        place["xh"], place["xl"] = x // 2, x % 2
        return place

    return permutation(target)


def send(value, pairs):
    return lax.ppermute(value, AXES, pairs)


def lon_ring(value, step):
    size = SIZES["z"] * SIZES["y"] * SIZES["xh"]
    return lax.ppermute(value, LON, [(i, (i + step) % size) for i in range(size)])


def lat_line(value, step):
    size = SIZES["xl"] * SIZES["core"]
    return lax.ppermute(
        value, LAT, [(i, i + step) for i in range(size) if 0 <= i + step < size]
    )


def after(value, *others):
    return lax.optimization_barrier((value,) + others)[0]


def ring_step(ahead, behind, axis):
    return send(ahead, along(axis, 1)), send(behind, along(axis, -1))


def gather_weights(w_qkv, w_out):
    core = lax.axis_index("core")
    x_hi = lax.axis_index("xh")
    shard = jnp.where(core == 0, w_qkv[:, : 2 * D], jnp.concatenate([w_qkv[:, 2 * D :], w_out], axis=1))
    other = send(shard, across_x())
    low = jnp.where(x_hi == 0, shard, other)
    high = jnp.where(x_hi == 0, other, shard)
    unit = jnp.concatenate([low, high])[None]
    first, second = unit[..., :CUT], unit[..., CUT:]

    found = []

    def keep(distances, column, block):
        found.append((distances, column, 0, block))
        found.append((distances, column, 1, send(block, along("core", 1))))

    sides = [send(first, along("y", s)) for s in Y_ORDER[1:]]
    z1, zm1 = ring_step(second, second, "z")
    first = jnp.concatenate([first] + sides)
    group = jnp.concatenate([second, z1, zm1])

    def keep_first(step, column, block):
        keep([(step, s) for s in Y_ORDER], column, block)

    def keep_second(zs, step, column, block):
        keep([(s, step) for s in zs], column, block)

    f1, fm1 = ring_step(first, first, "z")
    z2, zm2 = ring_step(z1, zm1, "z")
    g1, gm1 = ring_step(group, group, "y")
    keep_first(0, 0, first)
    keep_second((0, 1, -1), 0, CUT, group)
    z3, zm3 = ring_step(z2, zm2, "z")
    z4 = send(after(z3, f1, fm1), along("z", 1))
    f2, fm2 = ring_step(f1, fm1, "z")
    keep_first(1, 0, f1)
    keep_first(-1, 0, fm1)
    late = jnp.concatenate([z2, zm2, z3, zm3, z4])
    half = (2 * D - CUT) // 2
    g2 = send(g1[..., :half], along("y", 1))
    gm2 = send(gm1[..., half:], along("y", -1))
    zs = (0, 1, -1)
    keep_second(zs, 1, CUT, g1)
    keep_second(zs, -1, CUT, gm1)
    keep_second(zs, 2, CUT, g2)
    keep_second(zs, -2, CUT + half, gm2)
    zs = (2, -2, 3, -3, 4)
    l1, lm1 = ring_step(late, late, "y")
    keep_second(zs, 0, CUT, late)
    f3, fm3 = ring_step(f2, fm2, "z")
    keep_first(2, 0, f2)
    keep_first(-2, 0, fm2)
    l2 = send(l1[..., :half], along("y", 1))
    lm2 = send(lm1[..., half:], along("y", -1))
    f4 = send(f3[..., : CUT // 2], along("z", 1))
    fm4 = send(fm3[..., CUT // 2 :], along("z", -1))
    keep_first(3, 0, f3)
    keep_first(-3, 0, fm3)
    keep_second(zs, 1, CUT, l1)
    keep_second(zs, -1, CUT, lm1)
    keep_second(zs, 2, CUT, l2)
    keep_second(zs, -2, CUT + half, lm2)
    keep_first(4, 0, f4)
    keep_first(-4, CUT // 2, fm4)
    plan = [(tuple(distances), column, sibling) for distances, column, sibling, _ in found]
    return plan, [block for *_, block in found], sides[0]


def pull_ahead(tensor, early):
    edge = lon_ring(after(tensor[:, :, :SHIFT_LON], early), -1)
    widened = jnp.concatenate([tensor[:, :, SHIFT_LON:], edge], axis=2)
    rim = lat_line(widened[:, :SHIFT_LAT], -1)
    return jnp.concatenate([widened[:, SHIFT_LAT:], rim], axis=1)


def pull_behind(tensor):
    edge = lon_ring(tensor[:, :, -SHIFT_LON:], 1)
    widened = jnp.concatenate([edge, tensor[:, :, :-SHIFT_LON]], axis=2)
    rim = lat_line(widened[:, -SHIFT_LAT:], 1)
    return jnp.concatenate([rim, widened[:, :-SHIFT_LAT]], axis=1)


def mm(a, b):
    return lax.dot_general(a, b, (((1,), (0,)), ((), ())), preferred_element_type=jnp.float32)


def mm_nt(a, b):
    return lax.dot_general(a, b, (((1,), (1,)), ((), ())), preferred_element_type=jnp.float32)


def mm_tn(a, b):
    return lax.dot_general(a, b, (((0,), (0,)), ((), ())), preferred_element_type=jnp.float32)


def bf(value):
    return value.astype(jnp.bfloat16)


def sum_heads(value, ones):
    high = bf(value)
    low = bf(value - high.astype(jnp.float32))
    return mm(jnp.concatenate([high, low], axis=1), ones)


def window_kernel(plan, pos, xs, gs, mask, gain, scale, *refs):
    count = len(plan)
    blocks = refs[:count]
    upd, gwin = refs[count : count + 2]
    weights, normed, gatt, packed, attended, sem = refs[count + 2 :]
    z, y, core = pos[0], pos[1], pos[2]

    for (distances, column, sibling), block in zip(plan, blocks):
        side = lax.rem(core + sibling, 2)
        cols = pl.ds(column, block.shape[2])
        for j, (dz, dy) in enumerate(distances):
            unit = lax.rem(z - dz + 8, 8) * 4 + lax.rem(y - dy + 4, 4)
            pltpu.make_async_copy(block.at[j], weights.at[side, unit, :, cols], sem.at[side]).start()

    for i in range(4):
        rows = pl.ds(i * WIN, WIN)
        x = xs[rows, :].astype(jnp.float32)
        centre = x - jnp.mean(x, axis=-1, keepdims=True)
        spread = jnp.mean(centre * centre, axis=-1, keepdims=True)
        normed[rows, :] = bf(centre * lax.rsqrt(spread + 1e-05) * gain[...])

    for side in (1, 0):
        pltpu.make_async_copy(weights.at[side], weights.at[side], sem.at[side]).wait()

    @pl.loop(0, 2)
    def _(i):
        w = weights[1, pl.ds(i * 16, 16), :, D:].reshape(768, D)
        gatt[:, pl.ds(pl.multiple_of(i * 768, 128), 768)] = bf(mm_nt(gs[...], w))

    for m in range(3):

        @pl.loop(0, 3)
        def _(i, m=m):
            start = (m % 2) * D
            w = weights[m // 2, :, :, pl.ds(pl.multiple_of(start + i * 512, 128), 512)].reshape(D, 512)
            packed[:, pl.ds(pl.multiple_of(m * D + i * 512, 128), 512)] = bf(mm(normed[...], w))

    lane = lax.broadcasted_iota(jnp.int32, (256, 128), 1)
    row = lax.broadcasted_iota(jnp.int32, (256, 128), 0)
    same = (lane < 64) == (lax.rem(row, 128) < 64)
    ones = jnp.where(same, 1.0, 0.0).astype(jnp.bfloat16)
    left = lax.broadcasted_iota(jnp.int32, (WIN, 128), 1) < 64
    windows = [slice(i * WIN, (i + 1) * WIN) for i in range(4)]

    def spread_heads(block):
        zero = jnp.zeros_like(block)
        return jnp.concatenate([jnp.where(left, block, zero), jnp.where(left, zero, block)], axis=0)

    def fold_heads(block):
        return jnp.where(left, block[:WIN], block[WIN:])

    def each(function, *values):
        return jnp.concatenate([function(*[v[i] if isinstance(v, list) else v[part] for v in values]) for i, part in enumerate(windows)])

    @pl.loop(0, PAIRS)
    def _(p):
        at_q = pl.ds(pl.multiple_of(p * 128, 128), 128)
        at_k = pl.ds(pl.multiple_of(D + p * 128, 128), 128)
        at_v = pl.ds(pl.multiple_of(2 * D + p * 128, 128), 128)
        q = packed[:, at_q].astype(jnp.float32)
        k = packed[:, at_k].astype(jnp.float32)
        v = packed[:, at_v]
        d_out = gatt[:, at_q]
        factor = scale[pl.ds(p, 1), :]
        rq = lax.rsqrt(sum_heads(q * q, ones) + 1e-06)
        rk = lax.rsqrt(sum_heads(k * k, ones) + 1e-06)
        qn, kn = q * rq, k * rk
        qb, kb = bf(qn), bf(kn)
        k2 = [spread_heads(kb[part]) for part in windows]
        v2 = [spread_heads(v[part]) for part in windows]
        score = each(mm_nt, qb, k2)
        d_prob = each(mm_nt, d_out, v2)
        weight = jnp.exp(score * factor) * mask[...]
        prob = weight / sum_heads(weight, ones)
        prob16 = bf(prob)
        d_score = bf(prob * (d_prob - sum_heads(prob * d_prob, ones)) * factor)
        out = each(mm, prob16, v2)
        dv = each(lambda a, b: fold_heads(mm_tn(a, b)), prob16, d_out)
        dq = each(mm, d_score, k2)
        dk = each(lambda a, b: fold_heads(mm_tn(a, b)), d_score, qb)
        dq = rq * (dq - qn * sum_heads(qn * dq, ones))
        dk = rk * (dk - kn * sum_heads(kn * dk, ones))
        attended[:, at_q] = bf(out)
        packed[:, at_q] = bf(dq)
        packed[:, at_k] = bf(dk)
        packed[:, at_v] = bf(dv)

    @pl.loop(0, 3)
    def _(i):
        at = pl.ds(pl.multiple_of(i * 512, 128), 512)
        w = weights[1, :, :, pl.ds(pl.multiple_of(D + i * 512, 128), 512)].reshape(D, 512)
        upd[:, at] = bf(mm(attended[...], w))

    @pl.loop(0, 2)
    def _(i):
        unit = pl.ds(i * 16, 16)
        total = mm_nt(packed[:, : 2 * D], weights[0, unit].reshape(768, 2 * D))
        total += mm_nt(packed[:, 2 * D :], weights[1, unit, :, :D].reshape(768, D))
        gwin[:, pl.ds(pl.multiple_of(i * 768, 128), 768)] = bf(total)


def window_attention(pos, xs, gs, mask, gain, scale, plan, blocks):
    vmem = pl.BlockSpec(memory_space=pltpu.VMEM)
    return pl.pallas_call(
        functools.partial(window_kernel, plan),
        out_shape=[jax.ShapeDtypeStruct((TOK, D), jnp.bfloat16)] * 2,
        in_specs=[pl.BlockSpec(memory_space=pltpu.SMEM)]
        + [vmem] * 5
        + [pl.BlockSpec(memory_space=pl.ANY)] * len(blocks),
        out_specs=[vmem, vmem],
        scratch_shapes=[
            pltpu.VMEM((2, UNITS, UROWS, 2 * D), jnp.bfloat16),
            pltpu.VMEM((TOK, D), jnp.bfloat16),
            pltpu.VMEM((TOK, D), jnp.bfloat16),
            pltpu.VMEM((TOK, 3 * D), jnp.bfloat16),
            pltpu.VMEM((TOK, D), jnp.bfloat16),
            pltpu.SemaphoreType.DMA((2,)),
        ],
        compiler_params=pltpu.CompilerParams(vmem_limit_bytes=56 * 1024 * 1024),
        cost_estimate=pl.CostEstimate(
            flops=11 * 10**9, bytes_accessed=24 * 10**6, transcendentals=2 * 10**6
        ),
        name="window_attention",
    )(pos, xs, gs, mask, gain, scale, *blocks)


def finish_kernel(tokens, cotangent, update, grad, gain, out, grad_in):
    for i in range(4):
        rows = pl.ds(i * WIN, WIN)
        x = tokens[rows, :].astype(jnp.float32)
        out[rows, :] = bf(x + update[rows, :].astype(jnp.float32))
        centre = x - jnp.mean(x, axis=-1, keepdims=True)
        r = lax.rsqrt(jnp.mean(centre * centre, axis=-1, keepdims=True) + 1e-05)
        unit = centre * r
        g = grad[rows, :].astype(jnp.float32) * gain[...]
        pull = g - jnp.mean(g, axis=-1, keepdims=True)
        pull -= unit * jnp.mean(g * unit, axis=-1, keepdims=True)
        grad_in[rows, :] = bf(pull * r + cotangent[rows, :].astype(jnp.float32))


def finish(tokens, cotangent, update, grad, gain):
    vmem = pl.BlockSpec(memory_space=pltpu.VMEM)
    return pl.pallas_call(
        finish_kernel,
        out_shape=[jax.ShapeDtypeStruct((TOK, D), jnp.bfloat16)] * 2,
        in_specs=[vmem] * 5,
        out_specs=[vmem, vmem],
        compiler_params=pltpu.CompilerParams(vmem_limit_bytes=32 * 1024 * 1024),
        name="finish",
    )(tokens, cotangent, update, grad, gain)


def body(tokens, cotangent, gain, w_qkv, w_out, logit_scale, region_ids):
    lat, lon, _ = tokens.shape
    plan, blocks, early = gather_weights(w_qkv, w_out)
    shifted = pull_ahead(jnp.stack([tokens, cotangent]), early)
    shifted = shifted.reshape(2, TOK, D)
    gain = gain[None]
    scale = jnp.repeat(logit_scale, 64).reshape(PAIRS, 128)
    region = region_ids.reshape(4, WIN)
    row = lax.axis_index(LAT) * lat + lax.broadcasted_iota(jnp.int32, (lat, lon), 0)
    total_lat = lat * SIZES["xl"] * SIZES["core"]
    valid = (row + SHIFT_LAT < total_lat).reshape(4, WIN)
    allowed = (region[:, :, None] == region[:, None, :]) & (
        valid[:, None, :] | jnp.eye(WIN, dtype=bool)[None]
    )
    mask = allowed.astype(jnp.float32).reshape(TOK, WIN)
    mask = jnp.concatenate([mask, mask], axis=1)
    pos = jnp.stack([lax.axis_index("z"), lax.axis_index("y"), lax.axis_index("core")]).astype(jnp.int32)
    update, grad = window_attention(pos, shifted[0], shifted[1], mask, gain, scale, plan, blocks)
    update = pull_behind(update.reshape(1, lat, lon, D)).reshape(TOK, D)
    grad = pull_behind(grad.reshape(1, lat, lon, D)).reshape(TOK, D)
    output, grad_input = finish(
        tokens.reshape(TOK, D), cotangent.reshape(TOK, D), update, grad, gain
    )
    return output.reshape(lat, lon, D), grad_input.reshape(lat, lon, D)


def solution(mesh):
    fine = Mesh(mesh.devices.reshape(tuple(SIZES.values())), AXES)
    grid = P(LAT, LON, None)
    return jax.shard_map(
        body,
        mesh=fine,
        in_specs=(grid, grid, P(), P(LON, None), P(LON, None), P(), P(LAT, LON)),
        out_specs=(grid, grid),
        check_vma=False,
    )
```

```python
import functools
import itertools

import jax
import jax.numpy as jnp
from jax import lax
from jax.experimental import pallas as pl
from jax.experimental.pallas import tpu as pltpu
from jax.sharding import Mesh
from jax.sharding import PartitionSpec as P

SHIFT_LAT = 2
SHIFT_LON = 8
D = 1536
SIZES = {"xl": 2, "core": 2, "z": 8, "y": 4, "xh": 2}
AXES = tuple(SIZES)
LAT = ("xl", "core")
LON = ("z", "y", "xh")
TOK = 256
WIN = 64
PAIRS = 12
Y_ORDER = (0, 1, -1, 2)
UNITS = 32
UROWS = 48


def linear(place, axes):
    total = 0
    for axis in axes:
        total = total * SIZES[axis] + place[axis]
    return total


def permutation(target):
    pairs = []
    for values in itertools.product(*[range(SIZES[axis]) for axis in AXES]):
        place = dict(zip(AXES, values))
        goal = target(dict(place))
        if goal is not None:
            pairs.append((linear(place, AXES), linear(goal, AXES)))
    return pairs


def along(axis, step):
    def target(place):
        place[axis] = (place[axis] + step) % SIZES[axis]
        return place

    return permutation(target)


def across_x():
    def target(place):
        x = 3 - (place["xh"] * 2 + place["xl"])
        place["xh"], place["xl"] = x // 2, x % 2
        return place

    return permutation(target)


def send(value, pairs):
    return lax.ppermute(value, AXES, pairs)


def lon_ring(value, step):
    size = SIZES["z"] * SIZES["y"] * SIZES["xh"]
    return lax.ppermute(value, LON, [(i, (i + step) % size) for i in range(size)])


def lat_line(value, step):
    size = SIZES["xl"] * SIZES["core"]
    return lax.ppermute(
        value, LAT, [(i, i + step) for i in range(size) if 0 <= i + step < size]
    )


def after(value, *others):
    return lax.optimization_barrier((value,) + others)[0]


def ring_step(ahead, behind, axis):
    return send(ahead, along(axis, 1)), send(behind, along(axis, -1))


def gather_weights(w_qkv, w_out):
    core = lax.axis_index("core")
    x_hi = lax.axis_index("xh")
    first = jnp.where(core == 0, w_qkv[:, :D], w_qkv[:, 2 * D :])
    second = jnp.where(core == 0, w_qkv[:, D : 2 * D], w_out)

    def cross(block):
        other = send(block, across_x())
        low = jnp.where(x_hi == 0, block, other)
        high = jnp.where(x_hi == 0, other, block)
        return jnp.concatenate([low, high])[None]

    def far_ring(block, axis, reach):
        up = down = block
        got = [(0, 0, block)]
        for step in range(1, reach):
            up, down = ring_step(up, down, axis)
            got += [(step, 0, up), (-step, 0, down)]
        got.append((reach, 0, send(up[..., : D // 2], along(axis, 1))))
        got.append((-reach, D // 2, send(down[..., D // 2 :], along(axis, -1))))
        return got

    first, second = cross(first), cross(second)
    first = jnp.concatenate([first] + [send(first, along("y", s)) for s in Y_ORDER[1:]])
    up = down = second
    parts = [second]
    for _ in range(1, 4):
        up, down = ring_step(up, down, "z")
        parts += [up, down]
    parts.append(send(up, along("z", 1)))
    second = jnp.concatenate(parts)
    zs = (0, 1, -1, 2, -2, 3, -3, 4)
    found = [([(d, s) for s in Y_ORDER], c, b) for d, c, b in far_ring(first, "z", 4)]
    early = found[1][2]
    found += [([(s, d) for s in zs], D + c, b) for d, c, b in far_ring(second, "y", 2)]
    plan, blocks = [], []
    for distances, column, block in found:
        plan += [(tuple(distances), column, 0), (tuple(distances), column, 1)]
        blocks += [block, send(block, along("core", 1))]
    return plan, blocks, early


def pull_ahead(tensor, early):
    edge = lon_ring(after(tensor[:, :, :SHIFT_LON], early), -1)
    widened = jnp.concatenate([tensor[:, :, SHIFT_LON:], edge], axis=2)
    rim = lat_line(widened[:, :SHIFT_LAT], -1)
    return jnp.concatenate([widened[:, SHIFT_LAT:], rim], axis=1)


def pull_behind(tensor):
    lats, lons = SIZES["xl"] * SIZES["core"], SIZES["z"] * SIZES["y"] * SIZES["xh"]
    diagonal = [
        (a * lons + b, (a + 1) * lons + (b + 1) % lons) for a in range(lats - 1) for b in range(lons)
    ]
    edge = lon_ring(tensor[:, :-SHIFT_LAT, -SHIFT_LON:], 1)
    rim = lat_line(tensor[:, -SHIFT_LAT:, :-SHIFT_LON], 1)
    corner = send(tensor[:, -SHIFT_LAT:, -SHIFT_LON:], diagonal)
    upper = jnp.concatenate([corner, rim], axis=2)
    lower = jnp.concatenate([edge, tensor[:, :-SHIFT_LAT, :-SHIFT_LON]], axis=2)
    return jnp.concatenate([upper, lower], axis=1)


def mm(a, b):
    return lax.dot_general(a, b, (((1,), (0,)), ((), ())), preferred_element_type=jnp.float32)


def mm_nt(a, b):
    return lax.dot_general(a, b, (((1,), (1,)), ((), ())), preferred_element_type=jnp.float32)


def mm_tn(a, b):
    return lax.dot_general(a, b, (((0,), (0,)), ((), ())), preferred_element_type=jnp.float32)


def bf(value):
    return value.astype(jnp.bfloat16)


def sum_heads(value, ones):
    high = bf(value)
    low = bf(value - high.astype(jnp.float32))
    return mm(jnp.concatenate([high, low], axis=1), ones)


def window_kernel(plan, pos, xs, gs, mask, gain, scale, *refs):
    count = len(plan)
    blocks = refs[:count]
    result, weights, normed, gatt, packed, attended, sem = refs[count:]
    z, y, core = pos[0], pos[1], pos[2]

    for (distances, column, sibling), block in zip(plan, blocks):
        side = lax.rem(core + sibling, 2)
        cols = pl.ds(column, block.shape[2])
        for j, (dz, dy) in enumerate(distances):
            unit = lax.rem(z - dz + 8, 8) * 4 + lax.rem(y - dy + 4, 4)
            pltpu.make_async_copy(block.at[j], weights.at[side, unit, :, cols], sem.at[side]).start()

    for i in range(4):
        rows = pl.ds(i * WIN, WIN)
        x = xs[rows, :].astype(jnp.float32)
        centre = x - jnp.mean(x, axis=-1, keepdims=True)
        spread = jnp.mean(centre * centre, axis=-1, keepdims=True)
        normed[rows, :] = bf(centre * lax.rsqrt(spread + 1e-05) * gain[...])

    for side in (1, 0):
        pltpu.make_async_copy(weights.at[side], weights.at[side], sem.at[side]).wait()

    @pl.loop(0, 2)
    def _(i):
        w = weights[1, pl.ds(i * 16, 16), :, D:].reshape(768, D)
        gatt[:, pl.ds(pl.multiple_of(i * 768, 128), 768)] = bf(mm_nt(gs[...], w))

    for m in range(3):

        @pl.loop(0, 3)
        def _(i, m=m):
            start = (m % 2) * D
            w = weights[m // 2, :, :, pl.ds(pl.multiple_of(start + i * 512, 128), 512)].reshape(D, 512)
            packed[:, pl.ds(pl.multiple_of(m * D + i * 512, 128), 512)] = bf(mm(normed[...], w))

    lane = lax.broadcasted_iota(jnp.int32, (256, 128), 1)
    row = lax.broadcasted_iota(jnp.int32, (256, 128), 0)
    same = (lane < 64) == (lax.rem(row, 128) < 64)
    ones = jnp.where(same, 1.0, 0.0).astype(jnp.bfloat16)
    left = lax.broadcasted_iota(jnp.int32, (WIN, 128), 1) < 64
    windows = [slice(i * WIN, (i + 1) * WIN) for i in range(4)]

    def spread_heads(block):
        zero = jnp.zeros_like(block)
        return jnp.concatenate([jnp.where(left, block, zero), jnp.where(left, zero, block)], axis=0)

    def fold_heads(block):
        return jnp.where(left, block[:WIN], block[WIN:])

    def each(function, *values):
        return jnp.concatenate([function(*[v[i] if isinstance(v, list) else v[part] for v in values]) for i, part in enumerate(windows)])

    @pl.loop(0, PAIRS)
    def _(p):
        at_q = pl.ds(pl.multiple_of(p * 128, 128), 128)
        at_k = pl.ds(pl.multiple_of(D + p * 128, 128), 128)
        at_v = pl.ds(pl.multiple_of(2 * D + p * 128, 128), 128)
        q = packed[:, at_q].astype(jnp.float32)
        k = packed[:, at_k].astype(jnp.float32)
        v = packed[:, at_v]
        d_out = gatt[:, at_q]
        factor = scale[pl.ds(p, 1), :]
        rq = lax.rsqrt(sum_heads(q * q, ones) + 1e-06)
        rk = lax.rsqrt(sum_heads(k * k, ones) + 1e-06)
        qn, kn = q * rq, k * rk
        qb, kb = bf(qn), bf(kn)
        k2 = [spread_heads(kb[part]) for part in windows]
        v2 = [spread_heads(v[part]) for part in windows]
        score = each(mm_nt, qb, k2)
        d_prob = each(mm_nt, d_out, v2)
        weight = jnp.exp(score * factor) * mask[...]
        prob = weight / sum_heads(weight, ones)
        prob16 = bf(prob)
        d_score = bf(prob * (d_prob - sum_heads(prob * d_prob, ones)) * factor)
        out = each(mm, prob16, v2)
        dv = each(lambda a, b: fold_heads(mm_tn(a, b)), prob16, d_out)
        dq = each(mm, d_score, k2)
        dk = each(lambda a, b: fold_heads(mm_tn(a, b)), d_score, qb)
        dq = rq * (dq - qn * sum_heads(qn * dq, ones))
        dk = rk * (dk - kn * sum_heads(kn * dk, ones))
        attended[:, at_q] = bf(out)
        packed[:, at_q] = bf(dq)
        packed[:, at_k] = bf(dk)
        packed[:, at_v] = bf(dv)

    @pl.loop(0, 3)
    def _(i):
        at = pl.ds(pl.multiple_of(i * 512, 128), 512)
        w = weights[1, :, :, pl.ds(pl.multiple_of(D + i * 512, 128), 512)].reshape(D, 512)
        result[0, :, at] = bf(mm(attended[...], w))

    @pl.loop(0, 2)
    def _(i):
        unit = pl.ds(i * 16, 16)
        total = mm_nt(packed[:, : 2 * D], weights[0, unit].reshape(768, 2 * D))
        total += mm_nt(packed[:, 2 * D :], weights[1, unit, :, :D].reshape(768, D))
        result[1, :, pl.ds(pl.multiple_of(i * 768, 128), 768)] = bf(total)


def window_attention(pos, xs, gs, mask, gain, scale, plan, blocks):
    vmem = pl.BlockSpec(memory_space=pltpu.VMEM)
    return pl.pallas_call(
        functools.partial(window_kernel, plan),
        out_shape=jax.ShapeDtypeStruct((2, TOK, D), jnp.bfloat16),
        in_specs=[pl.BlockSpec(memory_space=pltpu.SMEM)]
        + [vmem] * 5
        + [pl.BlockSpec(memory_space=pl.ANY)] * len(blocks),
        out_specs=vmem,
        scratch_shapes=[
            pltpu.VMEM((2, UNITS, UROWS, 2 * D), jnp.bfloat16),
            pltpu.VMEM((TOK, D), jnp.bfloat16),
            pltpu.VMEM((TOK, D), jnp.bfloat16),
            pltpu.VMEM((TOK, 3 * D), jnp.bfloat16),
            pltpu.VMEM((TOK, D), jnp.bfloat16),
            pltpu.SemaphoreType.DMA((2,)),
        ],
        compiler_params=pltpu.CompilerParams(vmem_limit_bytes=56 * 1024 * 1024),
        cost_estimate=pl.CostEstimate(
            flops=11 * 10**9, bytes_accessed=24 * 10**6, transcendentals=2 * 10**6
        ),
        name="window_attention",
    )(pos, xs, gs, mask, gain, scale, *blocks)


def finish_kernel(tokens, cotangent, moved, gain, out, grad_in):
    for i in range(4):
        rows = pl.ds(i * WIN, WIN)
        x = tokens[rows, :].astype(jnp.float32)
        out[rows, :] = bf(x + moved[0, rows, :].astype(jnp.float32))
        centre = x - jnp.mean(x, axis=-1, keepdims=True)
        r = lax.rsqrt(jnp.mean(centre * centre, axis=-1, keepdims=True) + 1e-05)
        unit = centre * r
        g = moved[1, rows, :].astype(jnp.float32) * gain[...]
        pull = g - jnp.mean(g, axis=-1, keepdims=True)
        pull -= unit * jnp.mean(g * unit, axis=-1, keepdims=True)
        grad_in[rows, :] = bf(pull * r + cotangent[rows, :].astype(jnp.float32))


def finish(tokens, cotangent, moved, gain):
    vmem = pl.BlockSpec(memory_space=pltpu.VMEM)
    return pl.pallas_call(
        finish_kernel,
        out_shape=[jax.ShapeDtypeStruct((TOK, D), jnp.bfloat16)] * 2,
        in_specs=[vmem] * 4,
        out_specs=[vmem, vmem],
        compiler_params=pltpu.CompilerParams(vmem_limit_bytes=32 * 1024 * 1024),
        name="finish",
    )(tokens, cotangent, moved, gain)


def body(tokens, cotangent, gain, w_qkv, w_out, logit_scale, region_ids):
    lat, lon, _ = tokens.shape
    plan, blocks, early = gather_weights(w_qkv, w_out)
    shifted = pull_ahead(jnp.stack([tokens, cotangent]), early)
    shifted = shifted.reshape(2, TOK, D)
    gain = gain[None]
    scale = jnp.repeat(logit_scale, 64).reshape(PAIRS, 128)
    region = region_ids.reshape(4, WIN)
    row = lax.axis_index(LAT) * lat + lax.broadcasted_iota(jnp.int32, (lat, lon), 0)
    total_lat = lat * SIZES["xl"] * SIZES["core"]
    valid = (row + SHIFT_LAT < total_lat).reshape(4, WIN)
    allowed = (region[:, :, None] == region[:, None, :]) & (
        valid[:, None, :] | jnp.eye(WIN, dtype=bool)[None]
    )
    mask = allowed.astype(jnp.float32).reshape(TOK, WIN)
    mask = jnp.concatenate([mask, mask], axis=1)
    pos = jnp.stack([lax.axis_index("z"), lax.axis_index("y"), lax.axis_index("core")]).astype(jnp.int32)
    moved = window_attention(pos, shifted[0], shifted[1], mask, gain, scale, plan, blocks)
    moved = pull_behind(moved.reshape(2, lat, lon, D)).reshape(2, TOK, D)
    output, grad_input = finish(
        tokens.reshape(TOK, D), cotangent.reshape(TOK, D), moved, gain
    )
    return output.reshape(lat, lon, D), grad_input.reshape(lat, lon, D)


def solution(mesh):
    fine = Mesh(mesh.devices.reshape(tuple(SIZES.values())), AXES)
    grid = P(LAT, LON, None)
    return jax.shard_map(
        body,
        mesh=fine,
        in_specs=(grid, grid, P(), P(LON, None), P(LON, None), P(), P(LAT, LON)),
        out_specs=(grid, grid),
        check_vma=False,
    )
```

```python
import functools
import itertools

import jax
import jax.numpy as jnp
from jax import lax
from jax.experimental import pallas as pl
from jax.experimental.pallas import tpu as pltpu
from jax.sharding import Mesh
from jax.sharding import PartitionSpec as P

SHIFT_LAT = 2
SHIFT_LON = 8
D = 1536
SIZES = {"xl": 2, "core": 2, "z": 8, "y": 4, "xh": 2}
AXES = tuple(SIZES)
LAT = ("xl", "core")
LON = ("z", "y", "xh")
TOK = 256
WIN = 64
PAIRS = 12
Y_ORDER = (0, 1, -1, 2)
UNITS = 32
UROWS = 48


def linear(place, axes):
    total = 0
    for axis in axes:
        total = total * SIZES[axis] + place[axis]
    return total


def permutation(target):
    pairs = []
    for values in itertools.product(*[range(SIZES[axis]) for axis in AXES]):
        place = dict(zip(AXES, values))
        goal = target(dict(place))
        if goal is not None:
            pairs.append((linear(place, AXES), linear(goal, AXES)))
    return pairs


def along(axis, step):
    def target(place):
        place[axis] = (place[axis] + step) % SIZES[axis]
        return place

    return permutation(target)


def across_x():
    def target(place):
        x = 3 - (place["xh"] * 2 + place["xl"])
        place["xh"], place["xl"] = x // 2, x % 2
        return place

    return permutation(target)


def send(value, pairs):
    return lax.ppermute(value, AXES, pairs)


def lon_ring(value, step):
    size = SIZES["z"] * SIZES["y"] * SIZES["xh"]
    return lax.ppermute(value, LON, [(i, (i + step) % size) for i in range(size)])


def lat_line(value, step):
    size = SIZES["xl"] * SIZES["core"]
    return lax.ppermute(
        value, LAT, [(i, i + step) for i in range(size) if 0 <= i + step < size]
    )


def after(value, *others):
    return lax.optimization_barrier((value,) + others)[0]


def ring_step(ahead, behind, axis):
    return send(ahead, along(axis, 1)), send(behind, along(axis, -1))


def gather_weights(w_qkv, w_out):
    core = lax.axis_index("core")
    x_hi = lax.axis_index("xh")
    first = jnp.where(core == 0, w_qkv[:, :D], w_qkv[:, 2 * D :])
    second = jnp.where(core == 0, w_qkv[:, D : 2 * D], w_out)

    def cross(block):
        other = send(block, across_x())
        low = jnp.where(x_hi == 0, block, other)
        high = jnp.where(x_hi == 0, other, block)
        return jnp.concatenate([low, high])[None]

    def far_ring(block, axis, reach):
        up = down = block
        got = [(0, 0, block)]
        for step in range(1, reach):
            up, down = ring_step(up, down, axis)
            got += [(step, 0, up), (-step, 0, down)]
        got.append((reach, 0, send(up[..., : D // 2], along(axis, 1))))
        got.append((-reach, D // 2, send(down[..., D // 2 :], along(axis, -1))))
        return got

    first, second = cross(first), cross(second)
    first = jnp.concatenate([first] + [send(first, along("y", s)) for s in Y_ORDER[1:]])
    up = down = second
    parts = [second]
    for _ in range(1, 4):
        up, down = ring_step(up, down, "z")
        parts += [up, down]
    parts.append(send(up, along("z", 1)))
    second = jnp.concatenate(parts)
    zs = (0, 1, -1, 2, -2, 3, -3, 4)
    found = [([(d, s) for s in Y_ORDER], c, b) for d, c, b in far_ring(first, "z", 4)]
    early = found[1][2]
    found += [([(s, d) for s in zs], D + c, b) for d, c, b in far_ring(second, "y", 2)]
    plan, blocks = [], []
    for distances, column, block in found:
        plan += [(tuple(distances), column, 0), (tuple(distances), column, 1)]
        blocks += [block, send(block, along("core", 1))]
    return plan, blocks, early


def pull_ahead(tensor, early):
    edge = lon_ring(after(tensor[:, :, :SHIFT_LON], early), -1)
    widened = jnp.concatenate([tensor[:, :, SHIFT_LON:], edge], axis=2)
    rim = lat_line(widened[:, :SHIFT_LAT], -1)
    return jnp.concatenate([widened[:, SHIFT_LAT:], rim], axis=1)


def pull_behind(tensor):
    lats, lons = SIZES["xl"] * SIZES["core"], SIZES["z"] * SIZES["y"] * SIZES["xh"]
    diagonal = [
        (a * lons + b, (a + 1) * lons + (b + 1) % lons) for a in range(lats - 1) for b in range(lons)
    ]
    edge = lon_ring(tensor[:, :-SHIFT_LAT, -SHIFT_LON:], 1)
    rim = lat_line(tensor[:, -SHIFT_LAT:, :-SHIFT_LON], 1)
    corner = send(tensor[:, -SHIFT_LAT:, -SHIFT_LON:], diagonal)
    upper = jnp.concatenate([corner, rim], axis=2)
    lower = jnp.concatenate([edge, tensor[:, :-SHIFT_LAT, :-SHIFT_LON]], axis=2)
    return jnp.concatenate([upper, lower], axis=1)


def mm(a, b):
    return lax.dot_general(a, b, (((1,), (0,)), ((), ())), preferred_element_type=jnp.float32)


def mm_nt(a, b):
    return lax.dot_general(a, b, (((1,), (1,)), ((), ())), preferred_element_type=jnp.float32)


def mm_tn(a, b):
    return lax.dot_general(a, b, (((0,), (0,)), ((), ())), preferred_element_type=jnp.float32)


def bf(value):
    return value.astype(jnp.bfloat16)


def sum_heads(value, ones):
    high = bf(value)
    low = bf(value - high.astype(jnp.float32))
    return mm(jnp.concatenate([high, low], axis=1), ones)


def arrived(ref, sem):
    pltpu.make_async_copy(ref, ref, sem).wait()


def fetch(plan, blocks, weights, sem, z, y, core):
    def copy(sibling, side):
        for (distances, column, other), block in zip(plan, blocks):
            if other != sibling:
                continue
            cols = pl.ds(column, block.shape[2])
            for j, (dz, dy) in enumerate(distances):
                unit = lax.rem(z - dz + 8, 8) * 4 + lax.rem(y - dy + 4, 4)
                pltpu.make_async_copy(block.at[j], weights.at[side, unit, :, cols], sem.at[side]).start()

    for mine in (0, 1):

        @pl.when(core == mine)
        def _(mine=mine):
            copy(1 - mine, 1)
            copy(mine, 0)


def window_kernel(plan, pos, xs, gs, mask, gain, scale, *refs):
    count = len(plan)
    blocks = refs[:count]
    result, weights, normed, gatt, packed, attended, sem = refs[count:]
    z, y, core = pos[0], pos[1], pos[2]

    fetch(plan, blocks, weights, sem, z, y, core)

    for i in range(4):
        rows = pl.ds(i * WIN, WIN)
        x = xs[rows, :].astype(jnp.float32)
        centre = x - jnp.mean(x, axis=-1, keepdims=True)
        spread = jnp.mean(centre * centre, axis=-1, keepdims=True)
        normed[rows, :] = bf(centre * lax.rsqrt(spread + 1e-05) * gain[...])

    arrived(weights.at[1], sem.at[1])

    @pl.loop(0, 2)
    def _(i):
        w = weights[1, pl.ds(i * 16, 16), :, D:].reshape(768, D)
        gatt[:, pl.ds(pl.multiple_of(i * 768, 128), 768)] = bf(mm_nt(gs[...], w))

    for m in (2, 0, 1):
        if m == 0:
            arrived(weights.at[0], sem.at[0])

        @pl.loop(0, 3)
        def _(i, m=m):
            start = (m % 2) * D
            w = weights[m // 2, :, :, pl.ds(pl.multiple_of(start + i * 512, 128), 512)].reshape(D, 512)
            packed[:, pl.ds(pl.multiple_of(m * D + i * 512, 128), 512)] = bf(mm(normed[...], w))

    lane = lax.broadcasted_iota(jnp.int32, (256, 128), 1)
    row = lax.broadcasted_iota(jnp.int32, (256, 128), 0)
    same = (lane < 64) == (lax.rem(row, 128) < 64)
    ones = jnp.where(same, 1.0, 0.0).astype(jnp.bfloat16)
    left = lax.broadcasted_iota(jnp.int32, (WIN, 128), 1) < 64
    windows = [slice(i * WIN, (i + 1) * WIN) for i in range(4)]

    def spread_heads(block):
        zero = jnp.zeros_like(block)
        return jnp.concatenate([jnp.where(left, block, zero), jnp.where(left, zero, block)], axis=0)

    def fold_heads(block):
        return jnp.where(left, block[:WIN], block[WIN:])

    def each(function, *values):
        return jnp.concatenate([function(*[v[i] if isinstance(v, list) else v[part] for v in values]) for i, part in enumerate(windows)])

    @pl.loop(0, PAIRS)
    def _(p):
        at_q = pl.ds(pl.multiple_of(p * 128, 128), 128)
        at_k = pl.ds(pl.multiple_of(D + p * 128, 128), 128)
        at_v = pl.ds(pl.multiple_of(2 * D + p * 128, 128), 128)
        q = packed[:, at_q].astype(jnp.float32)
        k = packed[:, at_k].astype(jnp.float32)
        v = packed[:, at_v]
        d_out = gatt[:, at_q]
        factor = scale[pl.ds(p, 1), :]
        rq = lax.rsqrt(sum_heads(q * q, ones) + 1e-06)
        rk = lax.rsqrt(sum_heads(k * k, ones) + 1e-06)
        qn, kn = q * rq, k * rk
        qb, kb = bf(qn), bf(kn)
        k2 = [spread_heads(kb[part]) for part in windows]
        v2 = [spread_heads(v[part]) for part in windows]
        score = each(mm_nt, qb, k2)
        d_prob = each(mm_nt, d_out, v2)
        weight = jnp.exp(score * factor) * mask[...]
        prob = weight / sum_heads(weight, ones)
        prob16 = bf(prob)
        d_score = bf(prob * (d_prob - sum_heads(prob * d_prob, ones)) * factor)
        out = each(mm, prob16, v2)
        dv = each(lambda a, b: fold_heads(mm_tn(a, b)), prob16, d_out)
        dq = each(mm, d_score, k2)
        dk = each(lambda a, b: fold_heads(mm_tn(a, b)), d_score, qb)
        dq = rq * (dq - qn * sum_heads(qn * dq, ones))
        dk = rk * (dk - kn * sum_heads(kn * dk, ones))
        attended[:, at_q] = bf(out)
        packed[:, at_q] = bf(dq)
        packed[:, at_k] = bf(dk)
        packed[:, at_v] = bf(dv)

    @pl.loop(0, 3)
    def _(i):
        at = pl.ds(pl.multiple_of(i * 512, 128), 512)
        w = weights[1, :, :, pl.ds(pl.multiple_of(D + i * 512, 128), 512)].reshape(D, 512)
        result[0, :, at] = bf(mm(attended[...], w))

    @pl.loop(0, 2)
    def _(i):
        unit = pl.ds(i * 16, 16)
        total = mm_nt(packed[:, : 2 * D], weights[0, unit].reshape(768, 2 * D))
        total += mm_nt(packed[:, 2 * D :], weights[1, unit, :, :D].reshape(768, D))
        result[1, :, pl.ds(pl.multiple_of(i * 768, 128), 768)] = bf(total)


def window_attention(pos, xs, gs, mask, gain, scale, plan, blocks):
    vmem = pl.BlockSpec(memory_space=pltpu.VMEM)
    return pl.pallas_call(
        functools.partial(window_kernel, plan),
        out_shape=jax.ShapeDtypeStruct((2, TOK, D), jnp.bfloat16),
        in_specs=[pl.BlockSpec(memory_space=pltpu.SMEM)]
        + [vmem] * 5
        + [pl.BlockSpec(memory_space=pl.ANY)] * len(blocks),
        out_specs=vmem,
        scratch_shapes=[
            pltpu.VMEM((2, UNITS, UROWS, 2 * D), jnp.bfloat16),
            pltpu.VMEM((TOK, D), jnp.bfloat16),
            pltpu.VMEM((TOK, D), jnp.bfloat16),
            pltpu.VMEM((TOK, 3 * D), jnp.bfloat16),
            pltpu.VMEM((TOK, D), jnp.bfloat16),
            pltpu.SemaphoreType.DMA((2,)),
        ],
        compiler_params=pltpu.CompilerParams(vmem_limit_bytes=56 * 1024 * 1024),
        cost_estimate=pl.CostEstimate(
            flops=11 * 10**9, bytes_accessed=24 * 10**6, transcendentals=2 * 10**6
        ),
        name="window_attention",
    )(pos, xs, gs, mask, gain, scale, *blocks)


def finish_kernel(tokens, cotangent, moved, gain, out, grad_in):
    for i in range(4):
        rows = pl.ds(i * WIN, WIN)
        x = tokens[rows, :].astype(jnp.float32)
        out[rows, :] = bf(x + moved[0, rows, :].astype(jnp.float32))
        centre = x - jnp.mean(x, axis=-1, keepdims=True)
        r = lax.rsqrt(jnp.mean(centre * centre, axis=-1, keepdims=True) + 1e-05)
        unit = centre * r
        g = moved[1, rows, :].astype(jnp.float32) * gain[...]
        pull = g - jnp.mean(g, axis=-1, keepdims=True)
        pull -= unit * jnp.mean(g * unit, axis=-1, keepdims=True)
        grad_in[rows, :] = bf(pull * r + cotangent[rows, :].astype(jnp.float32))


def finish(tokens, cotangent, moved, gain):
    vmem = pl.BlockSpec(memory_space=pltpu.VMEM)
    return pl.pallas_call(
        finish_kernel,
        out_shape=[jax.ShapeDtypeStruct((TOK, D), jnp.bfloat16)] * 2,
        in_specs=[vmem] * 4,
        out_specs=[vmem, vmem],
        compiler_params=pltpu.CompilerParams(vmem_limit_bytes=32 * 1024 * 1024),
        name="finish",
    )(tokens, cotangent, moved, gain)


def body(tokens, cotangent, gain, w_qkv, w_out, logit_scale, region_ids):
    lat, lon, _ = tokens.shape
    plan, blocks, early = gather_weights(w_qkv, w_out)
    shifted = pull_ahead(jnp.stack([tokens, cotangent]), early)
    shifted = shifted.reshape(2, TOK, D)
    gain = gain[None]
    scale = jnp.repeat(logit_scale, 64).reshape(PAIRS, 128)
    region = region_ids.reshape(4, WIN)
    row = lax.axis_index(LAT) * lat + lax.broadcasted_iota(jnp.int32, (lat, lon), 0)
    total_lat = lat * SIZES["xl"] * SIZES["core"]
    valid = (row + SHIFT_LAT < total_lat).reshape(4, WIN)
    allowed = (region[:, :, None] == region[:, None, :]) & (
        valid[:, None, :] | jnp.eye(WIN, dtype=bool)[None]
    )
    mask = allowed.astype(jnp.float32).reshape(TOK, WIN)
    mask = jnp.concatenate([mask, mask], axis=1)
    pos = jnp.stack([lax.axis_index("z"), lax.axis_index("y"), lax.axis_index("core")]).astype(jnp.int32)
    moved = window_attention(pos, shifted[0], shifted[1], mask, gain, scale, plan, blocks)
    moved = pull_behind(moved.reshape(2, lat, lon, D)).reshape(2, TOK, D)
    output, grad_input = finish(
        tokens.reshape(TOK, D), cotangent.reshape(TOK, D), moved, gain
    )
    return output.reshape(lat, lon, D), grad_input.reshape(lat, lon, D)


def solution(mesh):
    fine = Mesh(mesh.devices.reshape(tuple(SIZES.values())), AXES)
    grid = P(LAT, LON, None)
    return jax.shard_map(
        body,
        mesh=fine,
        in_specs=(grid, grid, P(), P(LON, None), P(LON, None), P(), P(LAT, LON)),
        out_specs=(grid, grid),
        check_vma=False,
    )
```

```python
import functools
import itertools

import jax
import jax.numpy as jnp
from jax import lax
from jax.experimental import pallas as pl
from jax.experimental.pallas import tpu as pltpu
from jax.sharding import Mesh
from jax.sharding import PartitionSpec as P

SHIFT_LAT = 2
SHIFT_LON = 8
D = 1536
SIZES = {"xl": 2, "core": 2, "z": 8, "y": 4, "xh": 2}
AXES = tuple(SIZES)
LAT = ("xl", "core")
LON = ("z", "y", "xh")
TOK = 256
WIN = 64
PAIRS = 12
Y_ORDER = (0, 1, -1, 2)
UNITS = 32
UROWS = 48


def linear(place, axes):
    total = 0
    for axis in axes:
        total = total * SIZES[axis] + place[axis]
    return total


def permutation(target):
    pairs = []
    for values in itertools.product(*[range(SIZES[axis]) for axis in AXES]):
        place = dict(zip(AXES, values))
        goal = target(dict(place))
        if goal is not None:
            pairs.append((linear(place, AXES), linear(goal, AXES)))
    return pairs


def along(axis, step):
    def target(place):
        place[axis] = (place[axis] + step) % SIZES[axis]
        return place

    return permutation(target)


def across_x():
    def target(place):
        x = 3 - (place["xh"] * 2 + place["xl"])
        place["xh"], place["xl"] = x // 2, x % 2
        return place

    return permutation(target)


def send(value, pairs):
    return lax.ppermute(value, AXES, pairs)


def lon_ring(value, step):
    size = SIZES["z"] * SIZES["y"] * SIZES["xh"]
    return lax.ppermute(value, LON, [(i, (i + step) % size) for i in range(size)])


def lat_line(value, step):
    size = SIZES["xl"] * SIZES["core"]
    return lax.ppermute(
        value, LAT, [(i, i + step) for i in range(size) if 0 <= i + step < size]
    )


def after(value, *others):
    return lax.optimization_barrier((value,) + others)[0]


def ring_step(ahead, behind, axis):
    return send(ahead, along(axis, 1)), send(behind, along(axis, -1))


def gather_weights(w_qkv, w_out):
    core = lax.axis_index("core")
    x_hi = lax.axis_index("xh")
    first = jnp.where(core == 0, w_qkv[:, :D], w_qkv[:, 2 * D :])
    second = jnp.where(core == 0, w_qkv[:, D : 2 * D], w_out)

    def cross(block):
        other = send(block, across_x())
        low = jnp.where(x_hi == 0, block, other)
        high = jnp.where(x_hi == 0, other, block)
        return jnp.concatenate([low, high])[None]

    def far_ring(block, axis, reach):
        up = down = block
        got = [(0, 0, block)]
        for step in range(1, reach):
            up, down = ring_step(up, down, axis)
            got += [(step, 0, up), (-step, 0, down)]
        got.append((reach, 0, send(up[..., : D // 2], along(axis, 1))))
        got.append((-reach, D // 2, send(down[..., D // 2 :], along(axis, -1))))
        return got

    first, second = cross(first), cross(second)
    first = jnp.concatenate([first] + [send(first, along("y", s)) for s in Y_ORDER[1:]])
    up = down = second
    parts = [second]
    for _ in range(1, 4):
        up, down = ring_step(up, down, "z")
        parts += [up, down]
    parts.append(send(up, along("z", 1)))
    second = jnp.concatenate(parts)
    zs = (0, 1, -1, 2, -2, 3, -3, 4)
    found = [([(d, s) for s in Y_ORDER], c, b) for d, c, b in far_ring(first, "z", 4)]
    early = (found[1][2], found[2][2])
    found += [([(s, d) for s in zs], D + c, b) for d, c, b in far_ring(second, "y", 2)]
    plan, blocks = [], []
    for distances, column, block in found:
        plan += [(tuple(distances), column, 0), (tuple(distances), column, 1)]
        blocks += [block, send(block, along("core", 1))]
    return plan, blocks, early


def pull_ahead(tensor, early):
    edge = lon_ring(after(tensor[:, :, :SHIFT_LON], *early), -1)
    widened = jnp.concatenate([tensor[:, :, SHIFT_LON:], edge], axis=2)
    rim = lat_line(widened[:, :SHIFT_LAT], -1)
    return jnp.concatenate([widened[:, SHIFT_LAT:], rim], axis=1)


def pull_behind(tensor):
    lats, lons = SIZES["xl"] * SIZES["core"], SIZES["z"] * SIZES["y"] * SIZES["xh"]
    diagonal = [
        (a * lons + b, (a + 1) * lons + (b + 1) % lons) for a in range(lats - 1) for b in range(lons)
    ]
    edge = lon_ring(tensor[:, :-SHIFT_LAT, -SHIFT_LON:], 1)
    rim = lat_line(tensor[:, -SHIFT_LAT:, :-SHIFT_LON], 1)
    corner = send(tensor[:, -SHIFT_LAT:, -SHIFT_LON:], diagonal)
    upper = jnp.concatenate([corner, rim], axis=2)
    lower = jnp.concatenate([edge, tensor[:, :-SHIFT_LAT, :-SHIFT_LON]], axis=2)
    return jnp.concatenate([upper, lower], axis=1)


def mm(a, b):
    return lax.dot_general(a, b, (((1,), (0,)), ((), ())), preferred_element_type=jnp.float32)


def mm_nt(a, b):
    return lax.dot_general(a, b, (((1,), (1,)), ((), ())), preferred_element_type=jnp.float32)


def mm_tn(a, b):
    return lax.dot_general(a, b, (((0,), (0,)), ((), ())), preferred_element_type=jnp.float32)


def bf(value):
    return value.astype(jnp.bfloat16)


def sum_heads(value, ones):
    high = bf(value)
    low = bf(value - high.astype(jnp.float32))
    return mm(jnp.concatenate([high, low], axis=1), ones)


def arrived(ref, sem):
    pltpu.make_async_copy(ref, ref, sem).wait()


def fetch(plan, blocks, weights, sem, z, y, core):
    def copy(sibling, side):
        for (distances, column, other), block in zip(plan, blocks):
            if other != sibling:
                continue
            cols = pl.ds(column, block.shape[2])
            for j, (dz, dy) in enumerate(distances):
                unit = lax.rem(z - dz + 8, 8) * 4 + lax.rem(y - dy + 4, 4)
                pltpu.make_async_copy(block.at[j], weights.at[side, unit, :, cols], sem.at[side]).start()

    for mine in (0, 1):

        @pl.when(core == mine)
        def _(mine=mine):
            copy(1 - mine, 1)
            copy(mine, 0)


def window_kernel(plan, pos, xs, gs, mask, gain, scale, *refs):
    count = len(plan)
    blocks = refs[:count]
    result, weights, normed, gatt, packed, attended, sem = refs[count:]
    z, y, core = pos[0], pos[1], pos[2]

    fetch(plan, blocks, weights, sem, z, y, core)

    for i in range(4):
        rows = pl.ds(i * WIN, WIN)
        x = xs[rows, :].astype(jnp.float32)
        centre = x - jnp.mean(x, axis=-1, keepdims=True)
        spread = jnp.mean(centre * centre, axis=-1, keepdims=True)
        normed[rows, :] = bf(centre * lax.rsqrt(spread + 1e-05) * gain[...])

    arrived(weights.at[1], sem.at[1])

    @pl.loop(0, 2)
    def _(i):
        w = weights[1, pl.ds(i * 16, 16), :, D:].reshape(768, D)
        gatt[:, pl.ds(pl.multiple_of(i * 768, 128), 768)] = bf(mm_nt(gs[...], w))

    for m in (2, 0, 1):
        if m == 0:
            arrived(weights.at[0], sem.at[0])

        @pl.loop(0, 3)
        def _(i, m=m):
            start = (m % 2) * D
            w = weights[m // 2, :, :, pl.ds(pl.multiple_of(start + i * 512, 128), 512)].reshape(D, 512)
            packed[:, pl.ds(pl.multiple_of(m * D + i * 512, 128), 512)] = bf(mm(normed[...], w))

    lane = lax.broadcasted_iota(jnp.int32, (256, 128), 1)
    row = lax.broadcasted_iota(jnp.int32, (256, 128), 0)
    same = (lane < 64) == (lax.rem(row, 128) < 64)
    ones = jnp.where(same, 1.0, 0.0).astype(jnp.bfloat16)
    left = lax.broadcasted_iota(jnp.int32, (WIN, 128), 1) < 64
    windows = [slice(i * WIN, (i + 1) * WIN) for i in range(4)]

    def spread_heads(block):
        zero = jnp.zeros_like(block)
        return jnp.concatenate([jnp.where(left, block, zero), jnp.where(left, zero, block)], axis=0)

    def fold_heads(block):
        return jnp.where(left, block[:WIN], block[WIN:])

    def each(function, *values):
        return jnp.concatenate([function(*[v[i] if isinstance(v, list) else v[part] for v in values]) for i, part in enumerate(windows)])

    @pl.loop(0, PAIRS)
    def _(p):
        at_q = pl.ds(pl.multiple_of(p * 128, 128), 128)
        at_k = pl.ds(pl.multiple_of(D + p * 128, 128), 128)
        at_v = pl.ds(pl.multiple_of(2 * D + p * 128, 128), 128)
        q = packed[:, at_q].astype(jnp.float32)
        k = packed[:, at_k].astype(jnp.float32)
        v = packed[:, at_v]
        d_out = gatt[:, at_q]
        factor = scale[pl.ds(p, 1), :]
        rq = lax.rsqrt(sum_heads(q * q, ones) + 1e-06)
        rk = lax.rsqrt(sum_heads(k * k, ones) + 1e-06)
        qn, kn = q * rq, k * rk
        qb, kb = bf(qn), bf(kn)
        k2 = [spread_heads(kb[part]) for part in windows]
        v2 = [spread_heads(v[part]) for part in windows]
        score = each(mm_nt, qb, k2)
        d_prob = each(mm_nt, d_out, v2)
        weight = jnp.exp(score * factor) * mask[...]
        prob = weight / sum_heads(weight, ones)
        prob16 = bf(prob)
        d_score = bf(prob * (d_prob - sum_heads(prob * d_prob, ones)) * factor)
        out = each(mm, prob16, v2)
        dv = each(lambda a, b: fold_heads(mm_tn(a, b)), prob16, d_out)
        dq = each(mm, d_score, k2)
        dk = each(lambda a, b: fold_heads(mm_tn(a, b)), d_score, qb)
        dq = rq * (dq - qn * sum_heads(qn * dq, ones))
        dk = rk * (dk - kn * sum_heads(kn * dk, ones))
        attended[:, at_q] = bf(out)
        packed[:, at_q] = bf(dq)
        packed[:, at_k] = bf(dk)
        packed[:, at_v] = bf(dv)

    @pl.loop(0, 3)
    def _(i):
        at = pl.ds(pl.multiple_of(i * 512, 128), 512)
        w = weights[1, :, :, pl.ds(pl.multiple_of(D + i * 512, 128), 512)].reshape(D, 512)
        result[0, :, at] = bf(mm(attended[...], w))

    @pl.loop(0, 2)
    def _(i):
        unit = pl.ds(i * 16, 16)
        total = mm_nt(packed[:, : 2 * D], weights[0, unit].reshape(768, 2 * D))
        total += mm_nt(packed[:, 2 * D :], weights[1, unit, :, :D].reshape(768, D))
        result[1, :, pl.ds(pl.multiple_of(i * 768, 128), 768)] = bf(total)


def window_attention(pos, xs, gs, mask, gain, scale, plan, blocks):
    vmem = pl.BlockSpec(memory_space=pltpu.VMEM)
    return pl.pallas_call(
        functools.partial(window_kernel, plan),
        out_shape=jax.ShapeDtypeStruct((2, TOK, D), jnp.bfloat16),
        in_specs=[pl.BlockSpec(memory_space=pltpu.SMEM)]
        + [vmem] * 5
        + [pl.BlockSpec(memory_space=pl.ANY)] * len(blocks),
        out_specs=vmem,
        scratch_shapes=[
            pltpu.VMEM((2, UNITS, UROWS, 2 * D), jnp.bfloat16),
            pltpu.VMEM((TOK, D), jnp.bfloat16),
            pltpu.VMEM((TOK, D), jnp.bfloat16),
            pltpu.VMEM((TOK, 3 * D), jnp.bfloat16),
            pltpu.VMEM((TOK, D), jnp.bfloat16),
            pltpu.SemaphoreType.DMA((2,)),
        ],
        compiler_params=pltpu.CompilerParams(vmem_limit_bytes=56 * 1024 * 1024),
        cost_estimate=pl.CostEstimate(
            flops=11 * 10**9, bytes_accessed=24 * 10**6, transcendentals=2 * 10**6
        ),
        name="window_attention",
    )(pos, xs, gs, mask, gain, scale, *blocks)


def finish_kernel(tokens, cotangent, moved, gain, out, grad_in):
    for i in range(4):
        rows = pl.ds(i * WIN, WIN)
        x = tokens[rows, :].astype(jnp.float32)
        out[rows, :] = bf(x + moved[0, rows, :].astype(jnp.float32))
        centre = x - jnp.mean(x, axis=-1, keepdims=True)
        r = lax.rsqrt(jnp.mean(centre * centre, axis=-1, keepdims=True) + 1e-05)
        unit = centre * r
        g = moved[1, rows, :].astype(jnp.float32) * gain[...]
        pull = g - jnp.mean(g, axis=-1, keepdims=True)
        pull -= unit * jnp.mean(g * unit, axis=-1, keepdims=True)
        grad_in[rows, :] = bf(pull * r + cotangent[rows, :].astype(jnp.float32))


def finish(tokens, cotangent, moved, gain):
    vmem = pl.BlockSpec(memory_space=pltpu.VMEM)
    return pl.pallas_call(
        finish_kernel,
        out_shape=[jax.ShapeDtypeStruct((TOK, D), jnp.bfloat16)] * 2,
        in_specs=[vmem] * 4,
        out_specs=[vmem, vmem],
        compiler_params=pltpu.CompilerParams(vmem_limit_bytes=32 * 1024 * 1024),
        name="finish",
    )(tokens, cotangent, moved, gain)


def body(tokens, cotangent, gain, w_qkv, w_out, logit_scale, region_ids):
    lat, lon, _ = tokens.shape
    plan, blocks, early = gather_weights(w_qkv, w_out)
    shifted = pull_ahead(jnp.stack([tokens, cotangent]), early)
    shifted = shifted.reshape(2, TOK, D)
    gain = gain[None]
    scale = jnp.repeat(logit_scale, 64).reshape(PAIRS, 128)
    region = region_ids.reshape(4, WIN)
    row = lax.axis_index(LAT) * lat + lax.broadcasted_iota(jnp.int32, (lat, lon), 0)
    total_lat = lat * SIZES["xl"] * SIZES["core"]
    valid = (row + SHIFT_LAT < total_lat).reshape(4, WIN)
    allowed = (region[:, :, None] == region[:, None, :]) & (
        valid[:, None, :] | jnp.eye(WIN, dtype=bool)[None]
    )
    mask = allowed.astype(jnp.float32).reshape(TOK, WIN)
    mask = jnp.concatenate([mask, mask], axis=1)
    pos = jnp.stack([lax.axis_index("z"), lax.axis_index("y"), lax.axis_index("core")]).astype(jnp.int32)
    moved = window_attention(pos, shifted[0], shifted[1], mask, gain, scale, plan, blocks)
    moved = pull_behind(moved.reshape(2, lat, lon, D)).reshape(2, TOK, D)
    output, grad_input = finish(
        tokens.reshape(TOK, D), cotangent.reshape(TOK, D), moved, gain
    )
    return output.reshape(lat, lon, D), grad_input.reshape(lat, lon, D)


def solution(mesh):
    fine = Mesh(mesh.devices.reshape(tuple(SIZES.values())), AXES)
    grid = P(LAT, LON, None)
    return jax.shard_map(
        body,
        mesh=fine,
        in_specs=(grid, grid, P(), P(LON, None), P(LON, None), P(), P(LAT, LON)),
        out_specs=(grid, grid),
        check_vma=False,
    )
```
